512 devices in a mesh: lon: 64 (over x, z, y_hi), lat: 8 (over y_lo, core).
Axes of the slice: x: 4, y: 8 (y_hi: 2, y_lo: 4; y = y_hi * 4 + y_lo), z: 8, core: 2. Of those that a mesh axis runs over, the one named last changes fastest.
Arguments:
- fields: bfloat16 [128, 2880, 640], P('lat', 'lon'), may hold values from -6 to 6
- owner_slot: int32 [128], replicated, may hold values from 0 to 127, as said below
- widths: int32 [128], replicated, may hold values from 90 to 360, as said below
- tap_weights: bfloat16 [128, 2880], replicated, may hold values from -0.21875 to 0.21875
Outputs:
- filtered: bfloat16 [128, 2880, 640], P('lat', 'lon')
The draws below stay inside these ranges and needn't reach their ends.
Inputs may be any that keep to these rules, and one draw needn't show every extreme that they name: `owner_slot`: a permutation of the 128 rows; the 16 rows of each band of 16 rows are sent to every band of positions in equal numbers. `widths`: some row has the largest and some row the smallest value.
All inputs are finite; a program needn't handle non-finite values.
Results may differ from the reference program's by a relative error of at most 0.001.
Values may be sent and summed in bfloat16 or wider, within the bound.
A program may use at most 64 MiB of HBM per device.

```python
import jax
import jax.numpy as jnp
from jax import lax

NLON = 2880
CH = 640
LAT_DEV = 16
NLAT = 128


def draw_owner_slot(key, part):
    key = jax.random.fold_in(key, 11)
    bands = NLAT // LAT_DEV
    share = LAT_DEV // bands
    key_a, key_b = jax.random.split(key)
    perms = jax.vmap(lambda k: jax.random.permutation(k, LAT_DEV))(jax.random.split(key_a, bands))
    mixes = jax.vmap(lambda k: jax.random.permutation(k, LAT_DEV))(jax.random.split(key_b, bands))
    target = perms // share
    before = jnp.arange(bands, dtype=jnp.int32)[:, None] * share + perms % share
    within = mixes[target, before]
    return (target * LAT_DEV + within).reshape(-1).astype(jnp.int32)


def draw_widths(key, part):
    key = jax.random.fold_in(key, 13)
    key_a, key_b, key_c = jax.random.split(key, 3)
    lowest = NLON // 32
    highest = NLON // 8
    result = jax.random.randint(key_a, (NLAT,), lowest, highest + 1)
    first = jax.random.randint(key_b, (), 0, NLAT)
    second = (first + 1 + jax.random.randint(key_c, (), 0, NLAT - 1)) % NLAT
    result = result.at[first].set(highest).at[second].set(lowest)
    return result.astype(jnp.int32)


def level_of(stream_key, dims, shards, low, high):
    def one(axis_at, shards_of):
        draws = jax.random.uniform(jax.random.fold_in(jax.random.fold_in(stream_key, 6), axis_at), (shards_of,), jnp.float32, low / len(shards), high / len(shards))
        return jnp.repeat(jnp.exp(draws), dims[axis_at] // shards_of).reshape((-1,) + (1,) * (len(dims) - axis_at - 1))

    gain = one(*shards[0])
    for cut in shards[1:]:
        gain = gain * one(*cut)
    return gain


def noise(key, extent, deviation, limit, cuts=(), held_as=jnp.bfloat16):
    level = level_of(key, extent, cuts, -0.22, 0.18) if cuts else 1.0
    drawn = jax.random.normal(key, extent, jnp.float32) * deviation * level
    return jnp.minimum(jnp.maximum(drawn, -limit), limit).astype(held_as)


def setup_inputs(seed: int = 0) -> dict:
    splits = jax.random.split(jax.random.key(seed), 5)
    fields = noise(splits[0], (NLAT, NLON, CH), 1.0, 6.0, ((0, 8), (1, 64)))
    owner_slot = draw_owner_slot(jax.random.fold_in(splits[4], 71), 0)
    widths = draw_widths(jax.random.fold_in(splits[4], 71), 0)
    tap_weights = noise(splits[3], (NLAT, NLON), (NLON // 4) ** -0.5, 0.21875)
    return dict(fields=fields, owner_slot=owner_slot, widths=widths, tap_weights=tap_weights)


def reference(fields, owner_slot, widths, tap_weights):
    circle = fields.shape[1]
    offset = jnp.arange(circle, dtype=jnp.int32)
    distance = jnp.minimum(offset, circle - offset)
    active = jnp.where(distance[None, :] <= widths[:, None], tap_weights.astype(jnp.float32), jnp.zeros((), jnp.float32))

    def filter_row(pair):
        panel, weights = pair
        values = panel.astype(jnp.float32)
        spectrum = jnp.fft.rfft(values, axis=0)
        transfer = jnp.conj(jnp.fft.rfft(weights))
        convolved = jnp.fft.irfft(transfer[:, None] * spectrum, n=circle, axis=0)
        return (values + convolved).astype(jnp.bfloat16)

    smoothed = lax.map(filter_row, (fields, active))
    inverse = jnp.argsort(owner_slot).astype(jnp.int32)
    return smoothed[inverse]
```

```python
import jax
import jax.numpy as jnp
from jax import lax
from jax.experimental import pallas as pl
from jax.experimental.pallas import tpu as pltpu
from jax.sharding import PartitionSpec as P

MESH = pl.DeviceIdType.MESH

SECTOR = 45
PAD = 48
ROWS = 16
REACH = 360
CENTRE = 512
GROUP = 8
GROUP_K = GROUP + 16
CHUNKS = ((0, 640),)

BF16 = jnp.bfloat16
F32 = jnp.float32

ORDER = ((3, 0), (4, 0), (5, 1), (4, 1), (5, 0), (2, 0), (3, 1), (6, 1), (1, 0), (6, 0), (7, 1), (2, 1), (7, 0), (0, 0), (1, 1), (0, 1))


def div(a, b):
    return lax.div(a, jnp.int32(b))


def rem(a, b):
    return lax.rem(a, jnp.int32(b))


def device(x, z, y, c):
    return (x * 16 + z * 2 + div(y, 4), rem(y, 4) * 2 + c)


def job_of(z, y, c):
    shifted = rem(y + 6, 8)
    a, u = rem(shifted, 4), div(shifted, 4)
    return a, u, *destination(z, u, a, c)


def destination(z, u, a, c):
    b = rem(div(z, 2) + u + 2 * c + a, 4)
    to_core = rem(z + a, 2)
    return b, to_core


def kernel(owner, widths, fields, taps, out, *scratch):
    n = len(CHUNKS)
    per = [scratch[i * n:(i + 1) * n] for i in range(6)]
    outgoing, relay, window, done, back, landing = per
    toeplitz, tap_rows = scratch[6 * n:6 * n + 2]
    f1s, f1r, f2s, f2r, hs, hr, b1s, b1r, b2s, lr, tap_sem = scratch[6 * n + 2:]

    lon, lat = lax.axis_index("lon"), lax.axis_index("lat")
    x, z = div(lon, 16), rem(div(lon, 2), 8)
    y_hi, y_lo, c = rem(lon, 2), div(lat, 2), rem(lat, 2)
    y = y_hi * 4 + y_lo

    a, u, b, to_core = job_of(z, y, c)
    home = a * 2 + c

    tap_copy = pltpu.make_async_copy(taps.at[pl.ds(pl.multiple_of(home * ROWS, ROWS), ROWS), :], tap_rows, tap_sem)
    tap_copy.start()

    barrier = pltpu.get_barrier_semaphore()
    peers = 0
    for dy in range(8):
        for dc in range(2):
            if dy or dc:
                pl.semaphore_signal(barrier, inc=1, device_id=device(x, z, rem(y + dy, 8), rem(c + dc, 2)), device_id_type=MESH)
                peers += 1
    for dz in range(1, 8):
        pl.semaphore_signal(barrier, inc=1, device_id=device(x, rem(z + dz, 8), y, c), device_id_type=MESH)
        peers += 1
    for dx in (1, 3):
        pl.semaphore_signal(barrier, inc=1, device_id=device(rem(x + dx, 4), z, y, c), device_id_type=MESH)
        peers += 1

    to_band = [div(owner[lat * ROWS + j], ROWS) for j in range(ROWS)]
    code = []
    for j in range(ROWS):
        before = jnp.int32(0)
        for i in range(j):
            before = before + jnp.where(to_band[i] == to_band[j], 1, 0)
        code.append(to_band[j] * 2 + before)

    def stage(dz, side):
        to_z = rem(z + dz, 8)
        to_u = y_hi if side == 0 else 1 - y_hi
        to_b, core = destination(to_z, to_u, y_lo, c)
        wanted = (to_b * 2 + core) * 2 + to_u
        index = jnp.int32(0)
        for j in range(ROWS):
            index = index + jnp.where(code[j] == wanted, j, 0)
        t = dz * 2 + side
        index = jnp.minimum(index, ROWS - 1)
        for k, (lo, width) in enumerate(CHUNKS):
            outgoing[k][t, PAD - 16:, :] = jnp.zeros((16, width), BF16)
            outgoing[k][t, :SECTOR, :] = fields[index, :, lo:lo + width]

    def remote(src, dst, send, recv, dev):
        return pltpu.make_async_remote_copy(src_ref=src, dst_ref=dst, send_sem=send, recv_sem=recv, device_id=dev, device_id_type=MESH)

    sent = []

    def go(copy):
        copy.start()
        sent.append(copy)

    def y_to(side):
        return rem(y + (2 if side == 0 else 6), 8)

    def slot_of(src_z, src_y):
        return GROUP + src_z * 2 + div(src_y, 4)

    def forward_first(k, dz, side):
        t = dz * 2 + side
        src = outgoing[k].at[t]
        sem = k * 16 + t
        if dz == 0:
            go(remote(src, window[k].at[slot_of(z, y)], f2s.at[sem], f2r.at[sem], device(x, z, y_to(side), c)))
        elif dz % 2 == 0:
            go(remote(src, relay[k].at[t], f1s.at[sem], f1r.at[sem], device(x, z, y_to(side), c)))
        else:
            go(remote(src, relay[k].at[t], f1s.at[sem], f1r.at[sem], device(x, rem(z + dz, 8), y, c)))

    def forward_second(k, dz, side):
        if dz == 0:
            return
        t = dz * 2 + side
        sem = k * 16 + t
        here = relay[k].at[t]
        remote(here, here, f1s.at[sem], f1r.at[sem], device(x, z, y, c)).wait_recv()
        if dz % 2 == 0:
            src_y = rem(y + (6 if side == 0 else 2), 8)
            go(remote(here, window[k].at[slot_of(z, src_y)], f2s.at[sem], f2r.at[sem], device(x, rem(z + dz, 8), y, c)))
        else:
            src_z = rem(z + 8 - dz, 8)
            go(remote(here, window[k].at[slot_of(src_z, y)], f2s.at[sem], f2r.at[sem], device(x, z, y_to(side), c)))

    def halo(k, dz, side):
        t = dz * 2 + side
        sem = k * 16 + t
        src_z = rem(z + 8 - dz, 8)
        src_y = rem(y + (6 if side == 0 else 2), 8)
        slot = slot_of(src_z, src_y)
        here = window[k].at[slot]
        remote(here, here, f2s.at[sem], f2r.at[sem], device(x, z, y, c)).wait_recv()
        to_x = rem(x + 3 + 2 * div(src_z, 4), 4)
        go(remote(here, window[k].at[rem(slot + 16, 32)], hs.at[sem], hr.at[sem], device(to_x, z, y, c)))

    def halo_wait(k):
        for dz, side in ORDER:
            t = dz * 2 + side
            sem = k * 16 + t
            here = window[k].at[0]
            remote(here, here, hs.at[sem], hr.at[sem], device(x, z, y, c)).wait_recv()

    def toeplitz_of():
        tap_copy.wait()
        bands = [div(owner[home * ROWS + j], ROWS) for j in range(ROWS)]
        wanted = b * 2 + to_core
        seen, row = jnp.int32(0), jnp.int32(0)
        for j in range(ROWS):
            hit = jnp.where(bands[j] == wanted, 1, 0)
            row = row + jnp.where(seen == u, hit * j, 0)
            seen = seen + hit
        row = jnp.minimum(row, ROWS - 1)
        half = widths[home * ROWS + row]
        tap = tap_rows[...].astype(F32)
        pick = lax.broadcasted_iota(jnp.int32, tap.shape, 0) == row
        tap = jnp.sum(jnp.where(pick, tap, 0.0), axis=0, keepdims=True)
        tail = jnp.concatenate([tap[:, 2432:2880], jnp.zeros((1, 64), F32)], axis=1)
        tail = pltpu.roll(jnp.broadcast_to(tail, (8, 512)), 64, 1)[:1]
        line = jnp.concatenate([tail, tap[:, :512]], axis=1)
        offset = lax.broadcasted_iota(jnp.int32, line.shape, 1) - CENTRE
        line = jnp.where(jnp.abs(offset) <= half, line, 0.0)
        shifted = pltpu.roll(jnp.broadcast_to(line, (PAD, 1024)), 0, 1, stride=1, stride_axis=0)
        shifted = jnp.where(lax.broadcasted_iota(jnp.int32, shifted.shape, 0) < SECTOR, shifted, 0.0).astype(BF16)
        cols = GROUP_K * PAD
        col = lax.broadcasted_iota(jnp.int32, (1, cols), 1)
        sector = jnp.zeros_like(col)
        for d in range(1, GROUP_K):
            sector = sector + jnp.where(col >= PAD * d, 1, 0)
        within = col - sector * PAD
        source = jnp.where((within < SECTOR) & (sector < 17), sector * SECTOR + within + (CENTRE - REACH), -1)
        select = (lax.broadcasted_iota(jnp.int32, (1024, cols), 0) == source).astype(F32).astype(BF16)
        first = jnp.dot(shifted, select, preferred_element_type=F32)
        for s in range(GROUP):
            moved = first if s == 0 else pltpu.roll(first, PAD * s, 1)
            toeplitz[s * PAD:(s + 1) * PAD, :] = moved.astype(BF16)

    def compute(k):
        width = CHUNKS[k][1]
        for g in range(16 // GROUP):
            near = window[k][g * GROUP:g * GROUP + GROUP_K].reshape(GROUP_K * PAD, width)
            total = jnp.dot(toeplitz[...], near, preferred_element_type=F32)
            own = window[k][(g + 1) * GROUP:(g + 2) * GROUP].reshape(GROUP * PAD, width)
            total = own.astype(F32) + total
            done[k][g * GROUP:(g + 1) * GROUP] = total.astype(BF16).reshape(GROUP, PAD, width)

    unsent = []

    def here_or_there(src, dst, send, recv, to_y, core):
        stays = (to_y == y) & (core == c)
        copy = remote(src, dst, send, recv, device(x, z, to_y, core))

        @pl.when(stays)
        def _():
            pltpu.make_async_copy(src, dst, recv).start()

        @pl.when(jnp.logical_not(stays))
        def _():
            copy.start()

        unsent.append((stays, copy))

    def back_first(k, dz, side):
        sem = k * 16 + dz * 2 + side
        to_z = rem(z + dz, 8)
        here = done[k].at[to_z * 2 + side]
        if dz == 0:
            mine = home * 2 + u
            here_or_there(here, landing[k].at[mine], b1s.at[sem], lr.at[k * 16 + mine], b + 4 * side, to_core)
        elif dz % 2 == 0:
            place = 8 + div(a, 2) * 3 + dz // 2 - 1
            here_or_there(here, back[k].at[place], b1s.at[sem], b1r.at[k * 16 + place], b + 4 * side, to_core)
        else:
            place = side * 4 + dz // 2
            go(remote(here, back[k].at[place], b1s.at[sem], b1r.at[k * 16 + place], device(x, to_z, y, c)))

    def back_second(k, dz, side):
        if dz == 0:
            return
        sem = k * 16 + dz * 2 + side
        if dz % 2 == 0:
            place = 8 + side * 3 + dz // 2 - 1
            src_a = rem(c + z, 2) + 2 * side
            mix = rem(y_lo + 8 - div(z, 2) - src_a, 4)
            mine = (src_a * 2 + div(mix, 2)) * 2 + rem(mix, 2)
        else:
            place = side * 4 + dz // 2
            mine = home * 2 + u
        here = back[k].at[place]
        remote(here, here, b1s.at[sem], b1r.at[k * 16 + place], device(x, z, y, c)).wait_recv()
        there = landing[k].at[mine]
        arrived = lr.at[k * 16 + mine]
        if dz % 2 == 0:
            go(remote(here, there, b2s.at[sem], arrived, device(x, rem(z + dz, 8), y, c)))
        else:
            src_b, src_core = destination(rem(z + 8 - dz, 8), u, a, c)
            here_or_there(here, there, b2s.at[sem], arrived, src_b + 4 * side, src_core)

    def places():
        def add(band, found):
            found = list(found)
            seen = jnp.int32(0)
            for j in range(ROWS):
                at = owner[band * ROWS + j] - lat * ROWS
                for p in range(ROWS):
                    found[p] = found[p] + jnp.where(at == p, band * 2 + seen, 0)
                seen = seen + jnp.where((at >= 0) & (at < ROWS), 1, 0)
            return tuple(found)

        return lax.fori_loop(0, 8, add, (jnp.int32(0),) * ROWS)

    for dz, side in ORDER:
        stage(dz, side)
    pl.semaphore_wait(barrier, peers)
    for k in range(n):
        for dz, side in ORDER:
            forward_first(k, dz, side)
    toeplitz_of()
    for k in range(n):
        for dz, side in ORDER:
            forward_second(k, dz, side)
    found = places()
    for k in range(n):
        for dz, side in ORDER:
            halo(k, dz, side)
    for k in range(n):
        halo_wait(k)
        compute(k)
        for dz, side in ORDER:
            back_first(k, dz, side)
    for k in range(n):
        for dz, side in ORDER:
            back_second(k, dz, side)
    for k, (lo, width) in enumerate(CHUNKS):
        for mine in range(ROWS):
            here = landing[k].at[mine]
            remote(here, here, b2s.at[0], lr.at[k * 16 + mine], device(x, z, y, c)).wait_recv()
        for p in range(ROWS):
            out[p, :, lo:lo + width] = landing[k][jnp.minimum(found[p], ROWS - 1), :SECTOR, :]
    for copy in sent:
        copy.wait_send()
    for stays, copy in unsent:

        @pl.when(jnp.logical_not(stays))
        def _(copy=copy):
            copy.wait_send()


def body(fields, owner_slot, widths, tap_weights):
    n = len(CHUNKS)
    buffers = []
    for slots in (16, 16, 32, 16, 16, 16):
        buffers += [pltpu.VMEM((slots, PAD, width), BF16) for _, width in CHUNKS]
    return pl.pallas_call(
        kernel,
        out_shape=jax.ShapeDtypeStruct(fields.shape, BF16),
        in_specs=[
            pl.BlockSpec(memory_space=pltpu.SMEM),
            pl.BlockSpec(memory_space=pltpu.SMEM),
            pl.BlockSpec(memory_space=pltpu.VMEM),
            pl.BlockSpec(memory_space=pl.ANY),
        ],
        out_specs=pl.BlockSpec(memory_space=pltpu.VMEM),
        scratch_shapes=[
            *buffers,
            pltpu.VMEM((GROUP * PAD, GROUP_K * PAD), BF16),
            pltpu.VMEM((ROWS, tap_weights.shape[1]), BF16),
            *[pltpu.SemaphoreType.DMA((n * 16,)) for _ in range(10)],
            pltpu.SemaphoreType.DMA,
        ],
        compiler_params=pltpu.CompilerParams(collective_id=0, has_side_effects=True, vmem_limit_bytes=40 << 20),
    )(owner_slot, widths, fields, tap_weights)


def solution(mesh):
    in_specs = (P("lat", "lon", None), P(), P(), P())
    out_specs = P("lat", "lon", None)
    return jax.shard_map(body, mesh=mesh, in_specs=in_specs, out_specs=out_specs, check_vma=False)
```

```python
import jax
import jax.numpy as jnp
from jax import lax
from jax.experimental import pallas as pl
from jax.experimental.pallas import tpu as pltpu
from jax.sharding import PartitionSpec as P

MESH = pl.DeviceIdType.MESH

SECTOR = 45
PAD = 48
ROWS = 16
REACH = 360
CENTRE = 512
GROUP = 8
GROUP_K = GROUP + 16
CHUNKS = ((0, 384), (384, 256),)


ORDER = ((1, 0), (4, 1), (7, 1), (4, 0), (3, 1), (5, 0), (0, 0), (0, 1), (1, 1), (7, 0), (6, 1), (2, 1), (6, 0), (2, 0), (5, 1), (3, 0))

STEPS = {"A": "first", "R": "second", "H": "halo", "C": "filter", "S": "back", "F": "finish", "W": "weights", "P": "places"}
PLAN = ("A0.0", "W", "A0.1", "R0.0", "R0.1", "A1.1", "H0.0", "P", "A1.0", "H0.1", "R1.1", "R1.0", "C0", "H1.1", "H1.0", "S0.0", "C1", "S0.1", "S1.0", "S1.1", "F0", "F1")

BF16 = jnp.bfloat16
F32 = jnp.float32

def div(a, b):
    return lax.shift_right_logical(a, jnp.int32(b.bit_length() - 1))


def rem(a, b):
    return lax.bitwise_and(a, jnp.int32(b - 1))


def device(x, z, y, c):
    return (x * 16 + z * 2 + div(y, 4), rem(y, 4) * 2 + c)


def job_of(z, y, c):
    shifted = rem(y + 6, 8)
    a, u = rem(shifted, 4), div(shifted, 4)
    return a, u, *destination(z, u, a, c)


def destination(z, u, a, c):
    b = rem(div(z, 2) + u + 2 * c + a, 4)
    to_core = rem(z + a, 2)
    return b, to_core


def kernel(owner_in, widths_in, fields_in, taps, out, *scratch):
    n = len(CHUNKS)
    per = [scratch[i * n:(i + 1) * n] for i in range(6)]
    outgoing, relay, window, done, back, landing = per
    toeplitz, tap_rows, by_column, fields = scratch[6 * n:6 * n + 4]
    owner, widths, f1s, f1r, f2s, f2r, hs, hr, b1s, b1r, b2s, lr, tap_sem, owner_sem, width_sem, field_sem = scratch[6 * n + 4:]

    lon, lat = lax.axis_index("lon"), lax.axis_index("lat")
    x, z = div(lon, 16), rem(div(lon, 2), 8)
    y_hi, y_lo, c = rem(lon, 2), div(lat, 2), rem(lat, 2)
    y = y_hi * 4 + y_lo

    barrier = pltpu.get_barrier_semaphore()
    greeted = [device(x, rem(z + dz, 8), y, c) for dz in (4, 3, 5)]
    greeted += [device(x, z, rem(y + dy, 8), rem(c + dc, 2)) for dy in (4, 3, 5) for dc in range(2)]
    greeted += [device(x, rem(z + dz, 8), y, c) for dz in (2, 6)]
    greeted += [device(x, z, rem(y + dy, 8), rem(c + dc, 2)) for dy in (2, 6, 1, 7) for dc in range(2)]
    greeted += [device(x, rem(z + dz, 8), y, c) for dz in (1, 7)]
    greeted += [device(rem(x + dx, 4), z, y, c) for dx in (1, 3)] + [device(x, z, y, 1 - c)]
    for each in greeted:
        pl.semaphore_signal(barrier, inc=1, device_id=each, device_id_type=MESH)
    peers = len(greeted)

    a, u, b, to_core = job_of(z, y, c)
    home = a * 2 + c

    field_copies = [pltpu.make_async_copy(fields_in.at[pl.ds(i * 9, 9)], by_column.at[pl.ds(i * 9, 9)], field_sem.at[i]) for i in range(5)]
    tap_copy = pltpu.make_async_copy(taps, tap_rows, tap_sem)
    owner_copy = pltpu.make_async_copy(owner_in, owner, owner_sem)
    owner_copy.start()
    width_copy = pltpu.make_async_copy(widths_in, widths, width_sem)
    width_copy.start()
    for copy in field_copies:
        copy.start()

    tap_copy.start()
    owner_copy.wait()

    to_band = [div(owner[lat * ROWS + j], ROWS) for j in range(ROWS)]
    code = []
    for j in range(ROWS):
        before = jnp.int32(0)
        for i in range(j):
            before = before + jnp.where(to_band[i] == to_band[j], 1, 0)
        code.append(to_band[j] * 2 + before)

    def stage(dz, side):
        to_z = rem(z + dz, 8)
        to_u = y_hi if side == 0 else 1 - y_hi
        to_b, core = destination(to_z, to_u, y_lo, c)
        wanted = (to_b * 2 + core) * 2 + to_u
        index = jnp.int32(0)
        for j in range(ROWS):
            index = index + jnp.where(code[j] == wanted, j, 0)
        t = dz * 2 + side
        index = jnp.minimum(index, ROWS - 1)
        for k, (lo, width) in enumerate(CHUNKS):
            outgoing[k][t, PAD - 16:, :] = jnp.zeros((16, width), BF16)
            outgoing[k][t, :SECTOR, :] = fields[index, :SECTOR, lo:lo + width]

    def remote(src, dst, send, recv, dev):
        return pltpu.make_async_remote_copy(src_ref=src, dst_ref=dst, send_sem=send, recv_sem=recv, device_id=dev, device_id_type=MESH)

    sent = []

    def go(copy):
        copy.start()
        sent.append(copy)

    def y_to(side):
        return rem(y + (2 if side == 0 else 6), 8)

    def slot_of(src_z, src_y):
        return GROUP + src_z * 2 + div(src_y, 4)

    def forward_first(k, dz, side):
        t = dz * 2 + side
        src = outgoing[k].at[t]
        sem = k * 16 + t
        if dz == 0:
            go(remote(src, window[k].at[slot_of(z, y)], f2s.at[sem], f2r.at[sem], device(x, z, y_to(side), c)))
        elif dz % 2 == 0:
            go(remote(src, relay[k].at[t], f1s.at[sem], f1r.at[sem], device(x, z, y_to(side), c)))
        else:
            go(remote(src, relay[k].at[t], f1s.at[sem], f1r.at[sem], device(x, rem(z + dz, 8), y, c)))

    def forward_second(k, dz, side):
        if dz == 0:
            return
        t = dz * 2 + side
        sem = k * 16 + t
        here = relay[k].at[t]
        remote(here, here, f1s.at[sem], f1r.at[sem], device(x, z, y, c)).wait_recv()
        if dz % 2 == 0:
            src_y = rem(y + (6 if side == 0 else 2), 8)
            go(remote(here, window[k].at[slot_of(z, src_y)], f2s.at[sem], f2r.at[sem], device(x, rem(z + dz, 8), y, c)))
        else:
            src_z = rem(z + 8 - dz, 8)
            go(remote(here, window[k].at[slot_of(src_z, y)], f2s.at[sem], f2r.at[sem], device(x, z, y_to(side), c)))

    def halo(k, dz, side):
        t = dz * 2 + side
        sem = k * 16 + t
        src_z = rem(z + 8 - dz, 8)
        src_y = rem(y + (6 if side == 0 else 2), 8)
        slot = slot_of(src_z, src_y)
        here = window[k].at[slot]
        remote(here, here, f2s.at[sem], f2r.at[sem], device(x, z, y, c)).wait_recv()
        to_x = rem(x + 3 + 2 * div(src_z, 4), 4)
        go(remote(here, window[k].at[rem(slot + 16, 32)], hs.at[sem], hr.at[sem], device(to_x, z, y, c)))

    def halo_wait(k):
        for dz, side in ORDER:
            t = dz * 2 + side
            sem = k * 16 + t
            here = window[k].at[0]
            remote(here, here, hs.at[sem], hr.at[sem], device(x, z, y, c)).wait_recv()

    def toeplitz_of():
        tap_copy.wait()
        width_copy.wait()
        bands = [div(owner[home * ROWS + j], ROWS) for j in range(ROWS)]
        wanted = b * 2 + to_core
        seen, row = jnp.int32(0), jnp.int32(0)
        for j in range(ROWS):
            hit = jnp.where(bands[j] == wanted, 1, 0)
            row = row + jnp.where(seen == u, hit * j, 0)
            seen = seen + hit
        row = jnp.minimum(row, ROWS - 1)
        half = widths[home * ROWS + row]
        pick = (lax.broadcasted_iota(jnp.int32, (8, 128), 1) == home * ROWS + row).astype(F32).astype(BF16)
        tap = lax.dot_general(pick, tap_rows[...], (((1,), (1,)), ((), ())), preferred_element_type=F32)[:1]
        tail = jnp.concatenate([tap[:, 2432:2880], jnp.zeros((1, 64), F32)], axis=1)
        tail = pltpu.roll(jnp.broadcast_to(tail, (8, 512)), 64, 1)[:1]
        line = jnp.concatenate([tail, tap[:, :512]], axis=1)
        offset = lax.broadcasted_iota(jnp.int32, line.shape, 1) - CENTRE
        line = jnp.where(jnp.abs(offset) <= half, line, 0.0)
        shifted = pltpu.roll(jnp.broadcast_to(line, (PAD, 1024)), 0, 1, stride=1, stride_axis=0)
        shifted = jnp.where(lax.broadcasted_iota(jnp.int32, shifted.shape, 0) < SECTOR, shifted, 0.0)
        lane = lax.broadcasted_iota(jnp.int32, (PAD, 256), 1)
        columns = [jnp.zeros((PAD, 128), F32) for _ in range(GROUP_K * PAD // 128)]
        for d in range(17):
            old, new = CENTRE - REACH + SECTOR * d, PAD * d
            old_tile, new_tile = old // 128, new // 128
            old, new = old % 128, new % 128
            moved = pltpu.roll(shifted[:, old_tile * 128:old_tile * 128 + 256], (new - old) % 256, 1)
            moved = jnp.where((lane >= new) & (lane < new + SECTOR), moved, 0.0)
            columns[new_tile] = columns[new_tile] + moved[:, :128]
            if new + SECTOR > 128:
                columns[new_tile + 1] = columns[new_tile + 1] + moved[:, 128:]
        first = jnp.concatenate(columns, axis=1)
        for s in range(GROUP):
            moved = first if s == 0 else pltpu.roll(first, PAD * s, 1)
            toeplitz[s * PAD:(s + 1) * PAD, :] = moved.astype(BF16)

    def compute(k):
        width = CHUNKS[k][1]
        for g in range(16 // GROUP):
            near = window[k][g * GROUP:g * GROUP + GROUP_K].reshape(GROUP_K * PAD, width)
            total = jnp.dot(toeplitz[...], near, preferred_element_type=F32)
            own = window[k][(g + 1) * GROUP:(g + 2) * GROUP].reshape(GROUP * PAD, width)
            total = own.astype(F32) + total
            done[k][g * GROUP:(g + 1) * GROUP] = total.astype(BF16).reshape(GROUP, PAD, width)

    unsent = []

    def here_or_there(src, dst, send, recv, to_y, core):
        stays = (to_y == y) & (core == c)
        copy = remote(src, dst, send, recv, device(x, z, to_y, core))

        @pl.when(stays)
        def _():
            pltpu.make_async_copy(src, dst, recv).start()

        @pl.when(jnp.logical_not(stays))
        def _():
            copy.start()

        unsent.append((stays, copy))

    def back_first(k, dz, side):
        sem = k * 16 + dz * 2 + side
        to_z = rem(z + dz, 8)
        here = done[k].at[to_z * 2 + side]
        if dz == 0:
            mine = home * 2 + u
            here_or_there(here, landing[k].at[mine], b1s.at[sem], lr.at[k * 16 + mine], b + 4 * side, to_core)
        elif dz % 2 == 0:
            place = 8 + div(a, 2) * 3 + dz // 2 - 1
            here_or_there(here, back[k].at[place], b1s.at[sem], b1r.at[k * 16 + place], b + 4 * side, to_core)
        else:
            place = side * 4 + dz // 2
            go(remote(here, back[k].at[place], b1s.at[sem], b1r.at[k * 16 + place], device(x, to_z, y, c)))

    def back_second(k, dz, side):
        if dz == 0:
            return
        sem = k * 16 + dz * 2 + side
        if dz % 2 == 0:
            place = 8 + side * 3 + dz // 2 - 1
            src_a = rem(c + z, 2) + 2 * side
            mix = rem(y_lo + 8 - div(z, 2) - src_a, 4)
            mine = (src_a * 2 + div(mix, 2)) * 2 + rem(mix, 2)
        else:
            place = side * 4 + dz // 2
            mine = home * 2 + u
        here = back[k].at[place]
        remote(here, here, b1s.at[sem], b1r.at[k * 16 + place], device(x, z, y, c)).wait_recv()
        there = landing[k].at[mine]
        arrived = lr.at[k * 16 + mine]
        if dz % 2 == 0:
            go(remote(here, there, b2s.at[sem], arrived, device(x, rem(z + dz, 8), y, c)))
        else:
            src_b, src_core = destination(rem(z + 8 - dz, 8), u, a, c)
            here_or_there(here, there, b2s.at[sem], arrived, src_b + 4 * side, src_core)

    def places():
        slots = []
        for band in range(8):
            seen = jnp.int32(0)
            pair = [jnp.int32(0), jnp.int32(0)]
            for j in range(ROWS):
                at = owner[band * ROWS + j] - lat * ROWS
                mine = (at >= 0) & (at < ROWS)
                for r in range(2):
                    pair[r] = pair[r] + jnp.where(mine & (seen == r), at, 0)
                seen = seen + jnp.where(mine, 1, 0)
            slots += pair
        found = []
        for p in range(ROWS):
            place = jnp.int32(0)
            for mine, slot in enumerate(slots):
                place = place + jnp.where(slot == p, mine, 0)
            found.append(jnp.minimum(place, ROWS - 1))
        return found

    found = [None]

    def filter_chunk(k):
        halo_wait(k)
        compute(k)
        for dz, side in ORDER:
            back_first(k, dz, side)

    def finish(k):
        lo, width = CHUNKS[k]
        for mine in range(ROWS):
            here = landing[k].at[mine]
            remote(here, here, b2s.at[0], lr.at[k * 16 + mine], device(x, z, y, c)).wait_recv()
        for p in range(ROWS):
            out[p, :, lo:lo + width] = landing[k][found[0][p], :SECTOR, :]

    parts = {"first": forward_first, "second": forward_second, "halo": halo, "back": back_second}
    whole = {"filter": filter_chunk, "finish": finish}

    for copy in field_copies:
        copy.wait()
    fields[:, :SECTOR, :] = jnp.swapaxes(by_column[...], 0, 1)
    staged = [ORDER[0]]
    stage(*ORDER[0])
    pl.semaphore_wait(barrier, peers)
    for token in PLAN:
        name = STEPS[token[0]]
        if name == "weights":
            toeplitz_of()
        elif name == "places":
            found[0] = places()
        elif name in whole:
            whole[name](int(token[1]))
        else:
            start = 8 if token.endswith(".1") else 0
            stop = 8 if token.endswith(".0") else 16
            for message in ORDER[start:stop]:
                if message not in staged:
                    staged.append(message)
                    stage(*message)
                parts[name](int(token[1]), *message)

    for copy in sent:
        copy.wait_send()
    for stays, copy in unsent:

        @pl.when(jnp.logical_not(stays))
        def _(copy=copy):
            copy.wait_send()


def body(fields, owner_slot, widths, tap_weights):
    n = len(CHUNKS)
    buffers = []
    for slots in (16, 16, 32, 16, 16, 16):
        buffers += [pltpu.VMEM((slots, PAD, width), BF16) for _, width in CHUNKS]
    return pl.pallas_call(
        kernel,
        out_shape=jax.ShapeDtypeStruct(fields.shape, BF16),
        in_specs=[
            pl.BlockSpec(memory_space=pltpu.HBM),
            pl.BlockSpec(memory_space=pltpu.HBM),
            pl.BlockSpec(memory_space=pltpu.HBM),
            pl.BlockSpec(memory_space=pltpu.HBM),
        ],
        out_specs=pl.BlockSpec(memory_space=pltpu.VMEM),
        scratch_shapes=[
            *buffers,
            pltpu.VMEM((GROUP * PAD, GROUP_K * PAD), BF16),
            pltpu.VMEM(tap_weights.shape[::-1], BF16),
            pltpu.VMEM((SECTOR, ROWS, fields.shape[2]), BF16),
            pltpu.VMEM((ROWS, PAD, fields.shape[2]), BF16),
            pltpu.SMEM(owner_slot.shape, jnp.int32),
            pltpu.SMEM(widths.shape, jnp.int32),
            *[pltpu.SemaphoreType.DMA((n * 16,)) for _ in range(10)],
            *[pltpu.SemaphoreType.DMA for _ in range(3)],
            pltpu.SemaphoreType.DMA((5,)),
        ],
        compiler_params=pltpu.CompilerParams(collective_id=0, has_side_effects=True, vmem_limit_bytes=40 << 20),
    )(*[pltpu.with_memory_space_constraint(each, pltpu.HBM) for each in (owner_slot, widths, jnp.swapaxes(fields, 0, 1), tap_weights.T)])


def solution(mesh):
    in_specs = (P("lat", "lon", None), P(), P(), P())
    out_specs = P("lat", "lon", None)
    return jax.shard_map(body, mesh=mesh, in_specs=in_specs, out_specs=out_specs, check_vma=False)
```

```python
import jax
import jax.numpy as jnp
from jax import lax
from jax.experimental import pallas as pl
from jax.experimental.pallas import tpu as pltpu
from jax.sharding import PartitionSpec as P

MESH = pl.DeviceIdType.MESH

SECTOR = 45
PAD = 48
ROWS = 16
REACH = 360
CENTRE = 512
GROUP = 8
GROUP_K = GROUP + 16
CHUNKS = ((0, 384), (384, 256),)


ORDER = ((1, 0), (4, 1), (7, 1), (4, 0), (3, 1), (5, 0), (0, 0), (0, 1), (1, 1), (7, 0), (6, 1), (2, 1), (6, 0), (2, 0), (5, 1), (3, 0))

STEPS = {"A": "first", "R": "second", "H": "halo", "C": "filter", "S": "back", "F": "finish", "W": "weights", "P": "places", "D": "drain"}
PLAN = ("A0.0", "W", "A0.1", "R0.0", "R0.1", "A1.1", "H0.0", "P", "A1.0", "H0.1", "R1.1", "R1.0", "C0", "H1.1", "H1.0", "S0.0", "C1", "S0.1", "S1.0", "S1.1", "D0", "F0", "F1")

BF16 = jnp.bfloat16
F32 = jnp.float32

def div(a, b):
    return lax.shift_right_logical(a, jnp.int32(b.bit_length() - 1))


def rem(a, b):
    return lax.bitwise_and(a, jnp.int32(b - 1))


def device(x, z, y, c):
    return (x * 16 + z * 2 + div(y, 4), rem(y, 4) * 2 + c)


def job_of(z, y, c):
    shifted = rem(y + 6, 8)
    a, u = rem(shifted, 4), div(shifted, 4)
    return a, u, *destination(z, u, a, c)


def destination(z, u, a, c):
    b = rem(div(z, 2) + u + 2 * c + a, 4)
    to_core = rem(z + a, 2)
    return b, to_core


def kernel(owner_in, widths_in, fields_in, taps, out, *scratch):
    n = len(CHUNKS)
    per = [scratch[i * n:(i + 1) * n] for i in range(6)]
    outgoing, relay, window, done, back, landing = per
    toeplitz, tap_rows, by_column, fields = scratch[6 * n:6 * n + 4]
    owner, widths, f1s, f1r, f2s, f2r, hs, hr, b1s, b1r, b2s, lr, tap_sem, owner_sem, width_sem, field_sem = scratch[6 * n + 4:]

    lon, lat = lax.axis_index("lon"), lax.axis_index("lat")
    x, z = div(lon, 16), rem(div(lon, 2), 8)
    y_hi, y_lo, c = rem(lon, 2), div(lat, 2), rem(lat, 2)
    y = y_hi * 4 + y_lo

    barrier = pltpu.get_barrier_semaphore()
    greeted = [device(x, rem(z + dz, 8), y, c) for dz in (4, 3, 5)]
    greeted += [device(x, z, rem(y + dy, 8), rem(c + dc, 2)) for dy in (4, 3, 5) for dc in range(2)]
    greeted += [device(x, rem(z + dz, 8), y, c) for dz in (2, 6)]
    greeted += [device(x, z, rem(y + dy, 8), rem(c + dc, 2)) for dy in (2, 6, 1, 7) for dc in range(2)]
    greeted += [device(x, rem(z + dz, 8), y, c) for dz in (1, 7)]
    greeted += [device(rem(x + dx, 4), z, y, c) for dx in (1, 3)] + [device(x, z, y, 1 - c)]
    for each in greeted:
        pl.semaphore_signal(barrier, inc=1, device_id=each, device_id_type=MESH)
    peers = len(greeted)

    a, u, b, to_core = job_of(z, y, c)
    home = a * 2 + c

    field_copies = [pltpu.make_async_copy(fields_in.at[pl.ds(i * 9, 9)], by_column.at[pl.ds(i * 9, 9)], field_sem.at[i]) for i in range(5)]
    tap_copy = pltpu.make_async_copy(taps, tap_rows, tap_sem)
    owner_copy = pltpu.make_async_copy(owner_in, owner, owner_sem)
    owner_copy.start()
    width_copy = pltpu.make_async_copy(widths_in, widths, width_sem)
    width_copy.start()
    for copy in field_copies:
        copy.start()

    tap_copy.start()
    owner_copy.wait()

    to_band = [div(owner[lat * ROWS + j], ROWS) for j in range(ROWS)]
    code = []
    for j in range(ROWS):
        before = jnp.int32(0)
        for i in range(j):
            before = before + jnp.where(to_band[i] == to_band[j], 1, 0)
        code.append(to_band[j] * 2 + before)

    def stage(dz, side):
        to_z = rem(z + dz, 8)
        to_u = y_hi if side == 0 else 1 - y_hi
        to_b, core = destination(to_z, to_u, y_lo, c)
        wanted = (to_b * 2 + core) * 2 + to_u
        index = jnp.int32(0)
        for j in range(ROWS):
            index = index + jnp.where(code[j] == wanted, j, 0)
        t = dz * 2 + side
        index = jnp.minimum(index, ROWS - 1)
        for k, (lo, width) in enumerate(CHUNKS):
            outgoing[k][t, PAD - 16:, :] = jnp.zeros((16, width), BF16)
            outgoing[k][t, :SECTOR, :] = fields[index, :SECTOR, lo:lo + width]

    def remote(src, dst, send, recv, dev):
        return pltpu.make_async_remote_copy(src_ref=src, dst_ref=dst, send_sem=send, recv_sem=recv, device_id=dev, device_id_type=MESH)

    sent = []

    def go(copy):
        copy.start()
        sent.append((None, copy))

    def y_to(side):
        return rem(y + (2 if side == 0 else 6), 8)

    def slot_of(src_z, src_y):
        return GROUP + src_z * 2 + div(src_y, 4)

    def forward_first(k, dz, side):
        t = dz * 2 + side
        src = outgoing[k].at[t]
        sem = k * 16 + t
        if dz == 0:
            go(remote(src, window[k].at[slot_of(z, y)], f2s.at[sem], f2r.at[sem], device(x, z, y_to(side), c)))
        elif dz % 2 == 0:
            go(remote(src, relay[k].at[t], f1s.at[sem], f1r.at[sem], device(x, z, y_to(side), c)))
        else:
            go(remote(src, relay[k].at[t], f1s.at[sem], f1r.at[sem], device(x, rem(z + dz, 8), y, c)))

    def forward_second(k, dz, side):
        if dz == 0:
            return
        t = dz * 2 + side
        sem = k * 16 + t
        here = relay[k].at[t]
        remote(here, here, f1s.at[sem], f1r.at[sem], device(x, z, y, c)).wait_recv()
        if dz % 2 == 0:
            src_y = rem(y + (6 if side == 0 else 2), 8)
            go(remote(here, window[k].at[slot_of(z, src_y)], f2s.at[sem], f2r.at[sem], device(x, rem(z + dz, 8), y, c)))
        else:
            src_z = rem(z + 8 - dz, 8)
            go(remote(here, window[k].at[slot_of(src_z, y)], f2s.at[sem], f2r.at[sem], device(x, z, y_to(side), c)))

    def halo(k, dz, side):
        t = dz * 2 + side
        sem = k * 16 + t
        src_z = rem(z + 8 - dz, 8)
        src_y = rem(y + (6 if side == 0 else 2), 8)
        slot = slot_of(src_z, src_y)
        here = window[k].at[slot]
        remote(here, here, f2s.at[sem], f2r.at[sem], device(x, z, y, c)).wait_recv()
        to_x = rem(x + 3 + 2 * div(src_z, 4), 4)
        go(remote(here, window[k].at[rem(slot + 16, 32)], hs.at[sem], hr.at[sem], device(to_x, z, y, c)))

    def halo_wait(k):
        for dz, side in ORDER:
            t = dz * 2 + side
            sem = k * 16 + t
            here = window[k].at[0]
            remote(here, here, hs.at[sem], hr.at[sem], device(x, z, y, c)).wait_recv()

    def toeplitz_of():
        tap_copy.wait()
        width_copy.wait()
        bands = [div(owner[home * ROWS + j], ROWS) for j in range(ROWS)]
        wanted = b * 2 + to_core
        seen, row = jnp.int32(0), jnp.int32(0)
        for j in range(ROWS):
            hit = jnp.where(bands[j] == wanted, 1, 0)
            row = row + jnp.where(seen == u, hit * j, 0)
            seen = seen + hit
        row = jnp.minimum(row, ROWS - 1)
        half = widths[home * ROWS + row]
        pick = (lax.broadcasted_iota(jnp.int32, (8, 128), 1) == home * ROWS + row).astype(F32).astype(BF16)
        tap = lax.dot_general(pick, tap_rows[...], (((1,), (1,)), ((), ())), preferred_element_type=F32)[:1]
        tail = jnp.concatenate([tap[:, 2432:2880], jnp.zeros((1, 64), F32)], axis=1)
        tail = pltpu.roll(jnp.broadcast_to(tail, (8, 512)), 64, 1)[:1]
        line = jnp.concatenate([tail, tap[:, :512]], axis=1)
        offset = lax.broadcasted_iota(jnp.int32, line.shape, 1) - CENTRE
        line = jnp.where(jnp.abs(offset) <= half, line, 0.0)
        shifted = pltpu.roll(jnp.broadcast_to(line, (PAD, 1024)), 0, 1, stride=1, stride_axis=0)
        shifted = jnp.where(lax.broadcasted_iota(jnp.int32, shifted.shape, 0) < SECTOR, shifted, 0.0)
        lane = lax.broadcasted_iota(jnp.int32, (PAD, 256), 1)
        columns = [jnp.zeros((PAD, 128), F32) for _ in range(GROUP_K * PAD // 128)]
        for d in range(17):
            old, new = CENTRE - REACH + SECTOR * d, PAD * d
            old_tile, new_tile = old // 128, new // 128
            old, new = old % 128, new % 128
            moved = pltpu.roll(shifted[:, old_tile * 128:old_tile * 128 + 256], (new - old) % 256, 1)
            moved = jnp.where((lane >= new) & (lane < new + SECTOR), moved, 0.0)
            columns[new_tile] = columns[new_tile] + moved[:, :128]
            if new + SECTOR > 128:
                columns[new_tile + 1] = columns[new_tile + 1] + moved[:, 128:]
        first = jnp.concatenate(columns, axis=1)
        for s in range(GROUP):
            moved = first if s == 0 else pltpu.roll(first, PAD * s, 1)
            toeplitz[s * PAD:(s + 1) * PAD, :] = moved.astype(BF16)

    def compute(k):
        width = CHUNKS[k][1]
        for g in range(16 // GROUP):
            near = window[k][g * GROUP:g * GROUP + GROUP_K].reshape(GROUP_K * PAD, width)
            total = jnp.dot(toeplitz[...], near, preferred_element_type=F32)
            own = window[k][(g + 1) * GROUP:(g + 2) * GROUP].reshape(GROUP * PAD, width)
            total = own.astype(F32) + total
            done[k][g * GROUP:(g + 1) * GROUP] = total.astype(BF16).reshape(GROUP, PAD, width)

    def here_or_there(src, dst, send, recv, to_y, core):
        stays = (to_y == y) & (core == c)
        copy = remote(src, dst, send, recv, device(x, z, to_y, core))

        @pl.when(stays)
        def _():
            pltpu.make_async_copy(src, dst, recv).start()

        @pl.when(jnp.logical_not(stays))
        def _():
            copy.start()

        sent.append((stays, copy))

    def back_first(k, dz, side):
        sem = k * 16 + dz * 2 + side
        to_z = rem(z + dz, 8)
        here = done[k].at[to_z * 2 + side]
        if dz == 0:
            mine = home * 2 + u
            here_or_there(here, landing[k].at[mine], b1s.at[sem], lr.at[k * 16 + mine], b + 4 * side, to_core)
        elif dz % 2 == 0:
            place = 8 + div(a, 2) * 3 + dz // 2 - 1
            here_or_there(here, back[k].at[place], b1s.at[sem], b1r.at[k * 16 + place], b + 4 * side, to_core)
        else:
            place = side * 4 + dz // 2
            go(remote(here, back[k].at[place], b1s.at[sem], b1r.at[k * 16 + place], device(x, to_z, y, c)))

    def back_second(k, dz, side):
        if dz == 0:
            return
        sem = k * 16 + dz * 2 + side
        if dz % 2 == 0:
            place = 8 + side * 3 + dz // 2 - 1
            src_a = rem(c + z, 2) + 2 * side
            mix = rem(y_lo + 8 - div(z, 2) - src_a, 4)
            mine = (src_a * 2 + div(mix, 2)) * 2 + rem(mix, 2)
        else:
            place = side * 4 + dz // 2
            mine = home * 2 + u
        here = back[k].at[place]
        remote(here, here, b1s.at[sem], b1r.at[k * 16 + place], device(x, z, y, c)).wait_recv()
        there = landing[k].at[mine]
        arrived = lr.at[k * 16 + mine]
        if dz % 2 == 0:
            go(remote(here, there, b2s.at[sem], arrived, device(x, rem(z + dz, 8), y, c)))
        else:
            src_b, src_core = destination(rem(z + 8 - dz, 8), u, a, c)
            here_or_there(here, there, b2s.at[sem], arrived, src_b + 4 * side, src_core)

    def places():
        slots = []
        for band in range(8):
            seen = jnp.int32(0)
            pair = [jnp.int32(0), jnp.int32(0)]
            for j in range(ROWS):
                at = owner[band * ROWS + j] - lat * ROWS
                mine = (at >= 0) & (at < ROWS)
                for r in range(2):
                    pair[r] = pair[r] + jnp.where(mine & (seen == r), at, 0)
                seen = seen + jnp.where(mine, 1, 0)
            slots += pair
        found = []
        for p in range(ROWS):
            place = jnp.int32(0)
            for mine, slot in enumerate(slots):
                place = place + jnp.where(slot == p, mine, 0)
            found.append(jnp.minimum(place, ROWS - 1))
        return found

    found = [None]

    def filter_chunk(k):
        halo_wait(k)
        compute(k)
        for dz, side in ORDER:
            back_first(k, dz, side)

    def finish(k):
        lo, width = CHUNKS[k]
        for mine in range(ROWS):
            here = landing[k].at[mine]
            remote(here, here, b2s.at[0], lr.at[k * 16 + mine], device(x, z, y, c)).wait_recv()
        for p in range(ROWS):
            out[p, :, lo:lo + width] = landing[k][found[0][p], :SECTOR, :]

    parts = {"first": forward_first, "second": forward_second, "halo": halo, "back": back_second}
    whole = {"filter": filter_chunk, "finish": finish}

    def drain(keep):
        while len(sent) > keep:
            stays, copy = sent.pop(0)
            if stays is None:
                copy.wait_send()
            else:

                @pl.when(jnp.logical_not(stays))
                def _(copy=copy):
                    copy.wait_send()


    for copy in field_copies:
        copy.wait()
    fields[:, :SECTOR, :] = jnp.swapaxes(by_column[...], 0, 1)
    staged = [ORDER[0]]
    stage(*ORDER[0])
    pl.semaphore_wait(barrier, peers)
    for token in PLAN:
        name = STEPS[token[0]]
        if name == "weights":
            toeplitz_of()
        elif name == "places":
            found[0] = places()
        elif name == "drain":
            drain(int(token[1:]))
        elif name in whole:
            whole[name](int(token[1]))
        else:
            start = 8 if token.endswith(".1") else 0
            stop = 8 if token.endswith(".0") else 16
            for message in ORDER[start:stop]:
                if message not in staged:
                    staged.append(message)
                    stage(*message)
                parts[name](int(token[1]), *message)
    drain(0)


def body(fields, owner_slot, widths, tap_weights):
    n = len(CHUNKS)
    buffers = []
    for slots in (16, 16, 32, 16, 16, 16):
        buffers += [pltpu.VMEM((slots, PAD, width), BF16) for _, width in CHUNKS]
    return pl.pallas_call(
        kernel,
        out_shape=jax.ShapeDtypeStruct(fields.shape, BF16),
        in_specs=[
            pl.BlockSpec(memory_space=pltpu.HBM),
            pl.BlockSpec(memory_space=pltpu.HBM),
            pl.BlockSpec(memory_space=pltpu.HBM),
            pl.BlockSpec(memory_space=pltpu.HBM),
        ],
        out_specs=pl.BlockSpec(memory_space=pltpu.VMEM),
        scratch_shapes=[
            *buffers,
            pltpu.VMEM((GROUP * PAD, GROUP_K * PAD), BF16),
            pltpu.VMEM(tap_weights.shape[::-1], BF16),
            pltpu.VMEM((SECTOR, ROWS, fields.shape[2]), BF16),
            pltpu.VMEM((ROWS, PAD, fields.shape[2]), BF16),
            pltpu.SMEM(owner_slot.shape, jnp.int32),
            pltpu.SMEM(widths.shape, jnp.int32),
            *[pltpu.SemaphoreType.DMA((n * 16,)) for _ in range(10)],
            *[pltpu.SemaphoreType.DMA for _ in range(3)],
            pltpu.SemaphoreType.DMA((5,)),
        ],
        compiler_params=pltpu.CompilerParams(collective_id=0, has_side_effects=True, vmem_limit_bytes=40 << 20),
    )(*[pltpu.with_memory_space_constraint(each, pltpu.HBM) for each in (owner_slot, widths, jnp.swapaxes(fields, 0, 1), tap_weights.T)])


def solution(mesh):
    in_specs = (P("lat", "lon", None), P(), P(), P())
    out_specs = P("lat", "lon", None)
    return jax.shard_map(body, mesh=mesh, in_specs=in_specs, out_specs=out_specs, check_vma=False)
```
